32 devices in a mesh: layer: 4 (over y, x), tok: 8 (over z, core).
Axes of the slice: x: 2, y: 2, z: 4, core: 2. Of those that a mesh axis runs over, the one named last changes fastest.
Arguments:
- inputs: bfloat16 [4, 2048, 2048], P('layer', 'tok'), may hold values from -6 to 6
- enc_weight: bfloat16 [4, 2048, 1024], P(None, 'tok'), may hold values from -0.125 to 0.125
- enc_bias: float32 [4, 1024], replicated, may hold values from -0.5 to 0.5
- dec_weight: bfloat16 [10, 1024, 2048], P(None, 'tok'), may hold values from -0.1875 to 0.1875
- dec_bias: float32 [4, 2048], replicated, may hold values from -3 to 3
Outputs:
- rebuilt: bfloat16 [4, 1, 2048, 2048], P('layer', None, 'tok')
The draws below stay inside these ranges and needn't reach their ends.
All inputs are finite; a program needn't handle non-finite values.
Results may differ from the reference program's by a relative error of at most 0.0046.
Values may be sent and summed in bfloat16 or wider, within the bound.
A program may use at most 64 MiB of HBM per device.

```python
import jax
import jax.numpy as jnp

D = 2048
F = 1024
LAYERS = 4
COLS = 1
ROWS = 2048
PAIRS = 10
N_LAYER = 4


def levels(own_key, shape, split, least, top_value):
    loudness, own = 1.0, jax.random.fold_in(own_key, 6)
    for position, blocks in split:
        draws = jnp.exp(jax.random.uniform(jax.random.fold_in(own, position), (blocks,), jnp.float32, least / len(split), top_value / len(split)))
        loudness = loudness * jnp.repeat(draws, shape[position] // blocks).reshape([-1 if axis == position else 1 for axis in range(len(shape))])
    return loudness


def centred(key, shape, spread, reach, pieces=(), held_as=jnp.bfloat16):
    array = jax.random.normal(key, shape, jnp.float32) * spread
    if len(pieces) > 0:
        array = levels(key, shape, pieces, -0.22, 0.18) * array
    return jnp.clip(array, min=-reach, max=reach).astype(held_as)


def setup_inputs(seed: int = 0) -> dict:
    streams_of = jax.random.split(jax.random.key(seed), 6)
    return {
        "inputs": centred(streams_of[0], (N_LAYER, ROWS, D), 1.0, 6.0, ((0, 4), (1, 8))),
        "enc_weight": centred(streams_of[1], (LAYERS, D, F), D ** -0.5, 0.125, ((1, 8),)),
        "enc_bias": jnp.clip(jax.random.uniform(streams_of[2], (LAYERS, F), jnp.float32, -0.5, 0.5), -0.5, 0.5),
        "dec_weight": centred(streams_of[3], (PAIRS, F, D), F ** -0.5, 0.1875, ((1, 8),)),
        "dec_bias": centred(streams_of[4], (LAYERS, D), 0.5, 3.0, (), jnp.float32),
    }


def reference(inputs, enc_weight, enc_bias, dec_weight, dec_bias):
    stacked = inputs.reshape(LAYERS, COLS * ROWS, D)
    latent_list = []
    for layer_index in range(LAYERS):
        preact = jnp.dot(stacked[layer_index], enc_weight[layer_index], preferred_element_type=jnp.float32)
        latent_list.append(jnp.maximum(preact + enc_bias[layer_index].astype(jnp.float32), 0.0).astype(jnp.bfloat16))
    outputs = []
    for target in range(LAYERS):
        summed = jnp.zeros((COLS * ROWS, D), jnp.float32)
        for source in range(target + 1):
            summed = summed + jnp.dot(latent_list[source], dec_weight[target * (target + 1) // 2 + source], preferred_element_type=jnp.float32)
        rebuilt = (summed + dec_bias[target].astype(jnp.float32)).astype(jnp.bfloat16)
        rebuilt = rebuilt.reshape(COLS, ROWS, COLS, D // COLS).transpose(2, 0, 1, 3)
        outputs.append(rebuilt)
    return jnp.stack(outputs).reshape(N_LAYER, COLS, ROWS, D // COLS)
```

```python
import jax
import jax.numpy as jnp
from jax import lax
from jax.sharding import PartitionSpec as P


def body(inputs, enc_weight, enc_bias, dec_weight, dec_bias):
    layers = enc_weight.shape[0]
    positions = lax.axis_size("layer")
    col_groups = positions // layers
    position = lax.axis_index("layer")
    own_layer = position // col_groups
    token_rows = inputs[0]
    tok_count = token_rows.shape[0]
    latent_count = enc_weight.shape[2]
    width = dec_weight.shape[2] // positions

    own_encoder = lax.dynamic_index_in_dim(enc_weight, own_layer, 0, keepdims=False)
    preact = jnp.dot(
        token_rows,
        lax.all_gather(own_encoder, "tok", axis=0, tiled=True),
        preferred_element_type=jnp.float32,
    )
    own_bias = lax.dynamic_index_in_dim(enc_bias, own_layer, 0, keepdims=False)
    latents = jnp.maximum(preact + own_bias, 0.0).astype(jnp.bfloat16)
    gathered = lax.all_gather(latents[None], "layer", axis=0, tiled=True)
    grouped = gathered.reshape(layers, col_groups * tok_count, latent_count)

    own_slice = lax.dynamic_slice_in_dim(dec_weight, position * width, width, 2)
    bias_slice = lax.dynamic_slice_in_dim(dec_bias, position * width, width, 1)
    results = []
    for target in range(layers):
        first = target * (target + 1) // 2
        weights = lax.all_gather(own_slice[first : first + target + 1], "tok", axis=1, tiled=True)
        summed = jnp.zeros((col_groups * tok_count, width), jnp.float32)
        for source in range(target + 1):
            summed = summed + jnp.dot(grouped[source], weights[source], preferred_element_type=jnp.float32)
        results.append((summed + bias_slice[target]).astype(jnp.bfloat16))
    results = jnp.stack(results)

    r = position % layers
    pieces = []
    for step in range(layers):
        block = lax.dynamic_index_in_dim(results, (r + step) % layers, 0, keepdims=False)
        perm = [
            (p, (p % layers + step) % layers * col_groups + p // layers) for p in range(positions)
        ]
        pieces.append(block if col_groups == 1 and step == 0 else lax.ppermute(block, "layer", perm))
    stacked = jnp.stack(pieces)
    order = (own_layer - jnp.arange(layers)) % layers
    placed = jnp.concatenate([stacked[order[s]] for s in range(layers)], axis=1)
    return placed.reshape(col_groups, tok_count, layers * width)[None]


def solution(mesh):
    in_specs = (P("layer", "tok", None), P(None, "tok", None), P(), P(None, "tok", None), P())
    out_specs = P("layer", None, "tok", None)
    return jax.shard_map(body, mesh=mesh, in_specs=in_specs, out_specs=out_specs, check_vma=False)
```

```python
import functools

import jax
import jax.numpy as jnp
from jax import lax
from jax.experimental import pallas as pl
from jax.experimental.pallas import tpu as pltpu
from jax.sharding import PartitionSpec as P

MESH = pl.DeviceIdType.MESH


def kernel(
    positions, toks, layers,
    x_ref, enc_ref, enc_bias_ref, dec_ref, dec_bias_ref, out_ref,
    enc_buf, dec_buf, lat_buf, y_buf,
    own_sem, recv_sem, right_sem, left_sem, sibling_sem,
    lat_send, lat_recv, y_send, y_recv,
):
    groups = positions // layers
    chips = toks // 2
    me = lax.axis_index("layer")
    tok = lax.axis_index("tok")
    chip, core = tok // 2, tok % 2
    sibling = chip * 2 + 1 - core
    own_layer = me // groups
    enc_rows = enc_ref.shape[1]
    dec_rows = dec_ref.shape[1]
    width = dec_buf.shape[2]
    targets = list(range(layers))[::-1]
    chunks = layers + 1
    has_left, has_right = chip > 0, chip < chips - 1

    barrier = pltpu.get_barrier_semaphore()

    def greet(to):
        pl.semaphore_signal(barrier, inc=1, device_id=to, device_id_type=MESH)

    greet((me, sibling))
    for step in range(1, positions):
        greet((lax.rem(me + step, positions), tok))

    def part(chunk, slot):
        if chunk == 0:
            return enc_buf.at[pl.ds(pl.multiple_of(slot * enc_rows, enc_rows), enc_rows), :]
        target = targets[chunk - 1]
        first = target * (target + 1) // 2
        rows = pl.ds(pl.multiple_of(slot * dec_rows, dec_rows), dec_rows)
        return dec_buf.at[pl.ds(first, target + 1), rows, :]

    def load(chunk):
        if chunk == 0:
            source = enc_ref.at[own_layer]
        else:
            target = targets[chunk - 1]
            first = target * (target + 1) // 2
            columns = pl.ds(pl.multiple_of(me * width, width), width)
            source = dec_ref.at[pl.ds(first, target + 1), :, columns]
        return pltpu.make_async_copy(source, part(chunk, tok), own_sem.at[chunk])

    def send(chunk, slot, to, sems):
        return pltpu.make_async_remote_copy(
            src_ref=part(chunk, slot),
            dst_ref=part(chunk, slot),
            send_sem=sems.at[chunk, slot],
            recv_sem=recv_sem.at[chunk, slot],
            device_id=(me, to),
            device_id_type=MESH,
        )

    def to_right(chunk, slot):
        return send(chunk, slot, tok + 2, right_sem)

    def to_left(chunk, slot):
        return send(chunk, slot, tok - 2, left_sem)

    def to_sibling(chunk, slot):
        return send(chunk, slot, sibling, sibling_sem)

    for chunk in range(chunks):
        load(chunk).start()

    @pl.when(has_left)
    def _():
        greet((me, tok - 2))

    @pl.when(has_right)
    def _():
        greet((me, tok + 2))

    neighbours = has_left.astype(jnp.int32) + has_right.astype(jnp.int32)
    pl.semaphore_wait(barrier, positions + neighbours)

    def start_own(chunk):
        load(chunk).wait()

        @pl.when(has_right)
        def _():
            to_right(chunk, tok).start()

        @pl.when(has_left)
        def _():
            to_left(chunk, tok).start()

        to_sibling(chunk, tok).start()

    def forward(chunk):
        def step(distance, carry):
            @pl.when(chip - distance >= 0)
            def _():
                slot = tok - 2 * distance
                to_sibling(chunk, slot).wait_recv()

                @pl.when(has_right)
                def _():
                    to_right(chunk, slot).start()

                to_sibling(chunk, slot).start()

            @pl.when(chip + distance < chips)
            def _():
                slot = tok + 2 * distance
                to_sibling(chunk, slot).wait_recv()

                @pl.when(has_left)
                def _():
                    to_left(chunk, slot).start()

                to_sibling(chunk, slot).start()

            return carry

        lax.fori_loop(1, chips, step, 0)

    def wait_sibling(chunk):
        def step(index, carry):
            to_sibling(chunk, index * 2 + 1 - core).wait_recv()
            return carry

        lax.fori_loop(0, chips, step, 0)

    def drain(chunk):
        def step(index, carry):
            slot = index * 2 + core
            to_sibling(chunk, slot).wait_send()

            @pl.when(jnp.logical_and(has_right, index <= chip))
            def _():
                to_right(chunk, slot).wait_send()

            @pl.when(jnp.logical_and(has_left, index >= chip))
            def _():
                to_left(chunk, slot).wait_send()

            return carry

        lax.fori_loop(0, chips, step, 0)

    def lat_copy(step):
        return pltpu.make_async_remote_copy(
            src_ref=lat_buf.at[me],
            dst_ref=lat_buf.at[me],
            send_sem=lat_send.at[step],
            recv_sem=lat_recv.at[step],
            device_id=(lax.rem(me + step, positions), tok),
            device_id_type=MESH,
        )

    def encode():
        columns = enc_buf.shape[1]
        tile = min(256, columns)

        def step(index, carry):
            at = pl.ds(pl.multiple_of(index * tile, tile), tile)
            preact = jnp.dot(x_ref[...], enc_buf[:, at], preferred_element_type=jnp.float32)
            preact = preact + enc_bias_ref[pl.ds(own_layer, 1), at]
            lat_buf[me, :, at] = jnp.maximum(preact, 0.0).astype(lat_buf.dtype)
            return carry

        lax.fori_loop(0, columns // tile, step, 0)
        for step in range(1, positions):
            lat_copy(step).start()

    group, rank = me // layers, me % layers

    def y_dest(target):
        return target * groups + group

    def columns_of(slot):
        return pl.ds(pl.multiple_of(slot * width, width), width)

    def y_copy(target):
        return pltpu.make_async_remote_copy(
            src_ref=y_buf.at[target],
            dst_ref=out_ref.at[:, :, columns_of(rank)],
            send_sem=y_send.at[target],
            recv_sem=y_recv.at[rank],
            device_id=(y_dest(target), tok),
            device_id_type=MESH,
        )

    def y_keep(target):
        return pltpu.make_async_copy(
            y_buf.at[target], out_ref.at[:, :, columns_of(rank)], y_send.at[target]
        )

    def decode(target):
        first = target * (target + 1) // 2

        def step(index, carry):
            total = jnp.zeros((y_buf.shape[2], width), jnp.float32)
            for source in range(target + 1):
                total = total + jnp.dot(
                    lat_buf[source * groups + index],
                    dec_buf[first + source],
                    preferred_element_type=jnp.float32,
                )
            total = total + dec_bias_ref[target : target + 1, columns_of(me)]
            y_buf[target, index] = total.astype(y_buf.dtype)
            return carry

        lax.fori_loop(0, groups, step, 0)

        @pl.when(y_dest(target) == me)
        def _():
            y_keep(target).start()

        @pl.when(y_dest(target) != me)
        def _():
            y_copy(target).start()

    def compute(chunk):
        wait_sibling(chunk)
        if chunk == 0:
            encode()
            return
        if chunk == 1:
            for step in range(1, positions):
                lat_copy(step).wait_recv()
        decode(targets[chunk - 1])

    start_own(0)
    for chunk in range(chunks):
        if chunk + 1 < chunks:
            start_own(chunk + 1)
        forward(chunk)
        if chunk > 0:
            compute(chunk - 1)
    compute(chunks - 1)

    for target in range(layers):
        @pl.when(y_dest(target) == me)
        def _():
            y_keep(target).wait()

        @pl.when(y_dest(target) != me)
        def _():
            y_copy(target).wait_send()

    for slot in range(layers):
        @pl.when(lax.rem(me, groups) * layers + slot != me)
        def _():
            pltpu.make_async_remote_copy(
                src_ref=y_buf.at[0],
                dst_ref=out_ref.at[:, :, pl.ds(slot * width, width)],
                send_sem=y_send.at[0],
                recv_sem=y_recv.at[slot],
                device_id=(lax.rem(me + 1, positions), tok),
                device_id_type=MESH,
            ).wait_recv()

    for step in range(1, positions):
        lat_copy(step).wait_send()
    for chunk in range(chunks):
        drain(chunk)


def body(inputs, enc_weight, enc_bias, dec_weight, dec_bias):
    layers, enc_rows, latent_count = enc_weight.shape
    pairs, dec_rows, features = dec_weight.shape
    positions, toks = lax.axis_size("layer"), lax.axis_size("tok")
    groups = positions // layers
    tok_count = inputs.shape[1]
    width = features // positions
    chunks = layers + 1
    vmem = pl.BlockSpec(memory_space=pltpu.VMEM)
    hbm = pl.BlockSpec(memory_space=pltpu.HBM)
    dma = pltpu.SemaphoreType.DMA
    out = pl.pallas_call(
        functools.partial(kernel, positions, toks, layers),
        out_shape=jax.ShapeDtypeStruct((groups, tok_count, layers * width), jnp.bfloat16),
        in_specs=[vmem, hbm, vmem, hbm, vmem],
        out_specs=vmem,
        scratch_shapes=[
            pltpu.VMEM((enc_rows * toks, latent_count), jnp.bfloat16),
            pltpu.VMEM((pairs, dec_rows * toks, width), jnp.bfloat16),
            pltpu.VMEM((positions, tok_count, latent_count), jnp.bfloat16),
            pltpu.VMEM((layers, groups, tok_count, width), jnp.bfloat16),
            dma((chunks,)),
            dma((chunks, toks)),
            dma((chunks, toks)),
            dma((chunks, toks)),
            dma((chunks, toks)),
            dma((positions,)),
            dma((positions,)),
            dma((layers,)),
            dma((layers,)),
        ],
        compiler_params=pltpu.CompilerParams(
            collective_id=0, has_side_effects=True, vmem_limit_bytes=48 * 1024 * 1024
        ),
        cost_estimate=pl.CostEstimate(
            flops=2 * tok_count * latent_count * features * (1 + pairs // layers),
            bytes_accessed=8 * 1024 * 1024,
            transcendentals=0,
        ),
    )(inputs[0], enc_weight, enc_bias, dec_weight, dec_bias)
    return out[None]


def solution(mesh):
    in_specs = (P("layer", "tok", None), P(None, "tok", None), P(), P(None, "tok", None), P())
    out_specs = P("layer", None, "tok", None)
    return jax.shard_map(body, mesh=mesh, in_specs=in_specs, out_specs=out_specs, check_vma=False)
```

```python
import functools

import jax
import jax.numpy as jnp
from jax import lax
from jax.experimental import pallas as pl
from jax.experimental.pallas import tpu as pltpu
from jax.sharding import PartitionSpec as P

MESH = pl.DeviceIdType.MESH


def kernel(
    positions, toks, layers,
    x_ref, enc_ref, enc_bias_ref, dec_ref, dec_bias_ref, out_ref,
    x_buf, enc_buf, dec_buf, lat_buf, y_buf,
    own_sem, recv_sem, right_sem, left_sem, sibling_sem,
    x_send, x_recv, lat_send, lat_recv, y_send, y_recv,
):
    groups = positions // layers
    chips = toks // 2
    me = lax.axis_index("layer")
    tok = lax.axis_index("tok")
    chip, core = tok // 2, tok % 2
    sibling = chip * 2 + 1 - core
    own_layer = me // groups
    enc_rows = enc_ref.shape[1]
    dec_rows = dec_ref.shape[1]
    width = dec_buf.shape[2]
    targets = list(range(layers))[::-1]
    chunks = layers + 1
    has_left, has_right = chip > 0, chip < chips - 1

    folded = chips >= 4
    lowest, highest = (1, chips - 2) if folded else (0, chips - 1)
    is_worker = jnp.logical_and(chip >= lowest, chip <= highest)
    is_end = jnp.logical_not(is_worker)
    paired = jnp.logical_or(chip <= 1, chip >= chips - 2) if folded else chip < 0
    is_helper = jnp.logical_and(paired, is_worker)
    outwards = jnp.logical_or(chip == 0, chip == chips - 2)
    partner = tok + jnp.where(outwards, 2, -2)
    can_left, can_right = chip > lowest, chip < highest

    barrier = pltpu.get_barrier_semaphore()

    def greet(to):
        pl.semaphore_signal(barrier, inc=1, device_id=to, device_id_type=MESH)

    greet((me, sibling))
    for step in range(1, positions):
        greet((lax.rem(me + step, positions), tok))

    def part(chunk, slot):
        if chunk == 0:
            return enc_buf.at[pl.ds(pl.multiple_of(slot * enc_rows, enc_rows), enc_rows), :]
        target = targets[chunk - 1]
        first = target * (target + 1) // 2
        rows = pl.ds(pl.multiple_of(slot * dec_rows, dec_rows), dec_rows)
        return dec_buf.at[pl.ds(first, target + 1), rows, :]

    def load(chunk):
        if chunk == 0:
            source = enc_ref.at[own_layer]
        else:
            target = targets[chunk - 1]
            first = target * (target + 1) // 2
            columns = pl.ds(pl.multiple_of(me * width, width), width)
            source = dec_ref.at[pl.ds(first, target + 1), :, columns]
        return pltpu.make_async_copy(source, part(chunk, tok), own_sem.at[chunk])

    def send(chunk, slot, to, sems):
        return pltpu.make_async_remote_copy(
            src_ref=part(chunk, slot),
            dst_ref=part(chunk, slot),
            send_sem=sems.at[chunk, slot],
            recv_sem=recv_sem.at[chunk, slot],
            device_id=(me, to),
            device_id_type=MESH,
        )

    def to_right(chunk, slot):
        return send(chunk, slot, tok + 2, right_sem)

    def to_left(chunk, slot):
        return send(chunk, slot, tok - 2, left_sem)

    def to_sibling(chunk, slot):
        return send(chunk, slot, sibling, sibling_sem)

    def to_partner(chunk):
        return send(chunk, tok, partner, right_sem)

    def x_copy():
        return pltpu.make_async_remote_copy(
            src_ref=x_ref,
            dst_ref=x_buf,
            send_sem=x_send.at[0],
            recv_sem=x_recv.at[0],
            device_id=(me, partner),
            device_id_type=MESH,
        )

    for chunk in range(chunks):
        load(chunk).start()

    @pl.when(paired)
    def _():
        for step in range(1, positions):
            greet((lax.rem(me + step, positions), partner))

    @pl.when(has_left)
    def _():
        greet((me, tok - 2))

    @pl.when(has_right)
    def _():
        greet((me, tok + 2))

    neighbours = has_left.astype(jnp.int32) + has_right.astype(jnp.int32)
    crossing = paired.astype(jnp.int32) * (positions - 1)
    pl.semaphore_wait(barrier, positions + neighbours + crossing)

    def start_own(chunk):
        load(chunk).wait()

        @pl.when(can_right)
        def _():
            to_right(chunk, tok).start()

        @pl.when(can_left)
        def _():
            to_left(chunk, tok).start()

        to_sibling(chunk, tok).start()

    def forward(chunk):
        def step(distance, carry):
            @pl.when(chip - distance >= 0)
            def _():
                slot = tok - 2 * distance
                to_sibling(chunk, slot).wait_recv()

                @pl.when(can_right)
                def _():
                    to_right(chunk, slot).start()

                to_sibling(chunk, slot).start()

            @pl.when(chip + distance < chips)
            def _():
                slot = tok + 2 * distance
                to_sibling(chunk, slot).wait_recv()

                @pl.when(can_left)
                def _():
                    to_left(chunk, slot).start()

                to_sibling(chunk, slot).start()

            return carry

        lax.fori_loop(1, chips, step, 0)

    def wait_sibling(chunk):
        def step(index, carry):
            to_sibling(chunk, index * 2 + 1 - core).wait_recv()
            return carry

        lax.fori_loop(0, chips, step, 0)

    def drain(chunk):
        def step(index, carry):
            slot = index * 2 + core
            to_sibling(chunk, slot).wait_send()

            @pl.when(jnp.logical_and(can_right, index <= chip))
            def _():
                to_right(chunk, slot).wait_send()

            @pl.when(jnp.logical_and(can_left, index >= chip))
            def _():
                to_left(chunk, slot).wait_send()

            return carry

        lax.fori_loop(0, chips, step, 0)

    def lat_copy(part_of, step):
        return pltpu.make_async_remote_copy(
            src_ref=lat_buf.at[part_of, me],
            dst_ref=lat_buf.at[part_of, me],
            send_sem=lat_send.at[part_of, step],
            recv_sem=lat_recv.at[part_of, step],
            device_id=(lax.rem(me + step, positions), tok),
            device_id_type=MESH,
        )

    def encode(part_of):
        columns = enc_buf.shape[1]
        tile = min(256, columns)
        tokens = x_buf if part_of else x_ref

        def step(index, carry):
            at = pl.ds(pl.multiple_of(index * tile, tile), tile)
            preact = jnp.dot(tokens[...], enc_buf[:, at], preferred_element_type=jnp.float32)
            preact = preact + enc_bias_ref[pl.ds(own_layer, 1), at]
            lat_buf[part_of, me, :, at] = jnp.maximum(preact, 0.0).astype(lat_buf.dtype)
            return carry

        lax.fori_loop(0, columns // tile, step, 0)
        for step in range(1, positions):
            lat_copy(part_of, step).start()

    group, rank = me // layers, me % layers

    def y_dest(target):
        return target * groups + group

    def columns_of(slot):
        return pl.ds(pl.multiple_of(slot * width, width), width)

    def y_copy(part_of, target):
        return pltpu.make_async_remote_copy(
            src_ref=y_buf.at[part_of, target],
            dst_ref=out_ref.at[:, :, columns_of(rank)],
            send_sem=y_send.at[part_of, target],
            recv_sem=y_recv.at[rank],
            device_id=(y_dest(target), partner if part_of else tok),
            device_id_type=MESH,
        )

    def y_keep(target):
        return pltpu.make_async_copy(
            y_buf.at[0, target], out_ref.at[:, :, columns_of(rank)], y_send.at[0, target]
        )

    def decode(part_of, target):
        first = target * (target + 1) // 2

        def step(index, carry):
            total = jnp.zeros((y_buf.shape[3], width), jnp.float32)
            for source in range(target + 1):
                total = total + jnp.dot(
                    lat_buf[part_of, source * groups + index],
                    dec_buf[first + source],
                    preferred_element_type=jnp.float32,
                )
            total = total + dec_bias_ref[target : target + 1, columns_of(me)]
            y_buf[part_of, target, index] = total.astype(y_buf.dtype)
            return carry

        lax.fori_loop(0, groups, step, 0)

        if part_of:
            y_copy(part_of, target).start()
            return

        @pl.when(y_dest(target) == me)
        def _():
            y_keep(target).start()

        @pl.when(y_dest(target) != me)
        def _():
            y_copy(part_of, target).start()

    def compute(chunk, part_of):
        if chunk == 0:
            if part_of:
                x_copy().wait_recv()
            encode(part_of)
            return
        if chunk == 1:
            for step in range(1, positions):
                lat_copy(part_of, step).wait_recv()
        decode(part_of, targets[chunk - 1])

    def compute_both(chunk):
        wait_sibling(chunk)
        compute(chunk, 0)

        @pl.when(is_helper)
        def _():
            compute(chunk, 1)

    @pl.when(is_end)
    def _():
        sends = [to_partner(0), x_copy()] + [to_partner(chunk) for chunk in range(1, chunks)]
        loads = [load(0), None] + [load(chunk) for chunk in range(1, chunks)]
        for index in range(chunks + 1):
            if index >= 2:
                sends[index - 2].wait_send()
            if loads[index] is not None:
                loads[index].wait()
            sends[index].start()
        sends[chunks - 1].wait_send()
        sends[chunks].wait_send()

    @pl.when(is_worker)
    def _():
        start_own(0)
        begun = 1
        for chunk in range(chunks):
            ahead = min(chunks, chunk + (2 if chunk == 0 else 3))
            for later in range(begun, ahead):
                start_own(later)
            begun = max(begun, ahead)
            forward(chunk)
            if chunk > 0:
                compute_both(chunk - 1)
        compute_both(chunks - 1)

        for target in range(layers):
            @pl.when(y_dest(target) == me)
            def _():
                y_keep(target).wait()

            @pl.when(y_dest(target) != me)
            def _():
                y_copy(0, target).wait_send()

    for slot in range(layers):
        @pl.when(jnp.logical_or(is_end, lax.rem(me, groups) * layers + slot != me))
        def _():
            pltpu.make_async_remote_copy(
                src_ref=y_buf.at[0, 0],
                dst_ref=out_ref.at[:, :, pl.ds(slot * width, width)],
                send_sem=y_send.at[0, 0],
                recv_sem=y_recv.at[slot],
                device_id=(lax.rem(me + 1, positions), tok),
                device_id_type=MESH,
            ).wait_recv()

    @pl.when(is_worker)
    def _():
        for step in range(1, positions):
            lat_copy(0, step).wait_send()
        for chunk in range(chunks):
            drain(chunk)

    @pl.when(is_helper)
    def _():
        for step in range(1, positions):
            lat_copy(1, step).wait_send()
        for target in range(layers):
            y_copy(1, target).wait_send()


def body(inputs, enc_weight, enc_bias, dec_weight, dec_bias):
    layers, enc_rows, latent_count = enc_weight.shape
    pairs, dec_rows, features = dec_weight.shape
    positions, toks = lax.axis_size("layer"), lax.axis_size("tok")
    groups = positions // layers
    tok_count = inputs.shape[1]
    width = features // positions
    chunks = layers + 1
    vmem = pl.BlockSpec(memory_space=pltpu.VMEM)
    hbm = pl.BlockSpec(memory_space=pltpu.HBM)
    dma = pltpu.SemaphoreType.DMA
    out = pl.pallas_call(
        functools.partial(kernel, positions, toks, layers),
        out_shape=jax.ShapeDtypeStruct((groups, tok_count, layers * width), jnp.bfloat16),
        in_specs=[vmem, hbm, vmem, hbm, vmem],
        out_specs=vmem,
        scratch_shapes=[
            pltpu.VMEM((tok_count, enc_rows * toks), jnp.bfloat16),
            pltpu.VMEM((enc_rows * toks, latent_count), jnp.bfloat16),
            pltpu.VMEM((pairs, dec_rows * toks, width), jnp.bfloat16),
            pltpu.VMEM((2, positions, tok_count, latent_count), jnp.bfloat16),
            pltpu.VMEM((2, layers, groups, tok_count, width), jnp.bfloat16),
            dma((chunks,)),
            dma((chunks, toks)),
            dma((chunks, toks)),
            dma((chunks, toks)),
            dma((chunks, toks)),
            dma((1,)),
            dma((1,)),
            dma((2, positions)),
            dma((2, positions)),
            dma((2, layers)),
            dma((layers,)),
        ],
        compiler_params=pltpu.CompilerParams(
            collective_id=0, has_side_effects=True, vmem_limit_bytes=58 * 1024 * 1024
        ),
        cost_estimate=pl.CostEstimate(
            flops=2 * tok_count * latent_count * features * (1 + pairs // layers),
            bytes_accessed=8 * 1024 * 1024,
            transcendentals=0,
        ),
    )(inputs[0], enc_weight, enc_bias, dec_weight, dec_bias)
    return out[None]


def solution(mesh):
    in_specs = (P("layer", "tok", None), P(None, "tok", None), P(), P(None, "tok", None), P())
    out_specs = P("layer", None, "tok", None)
    return jax.shard_map(body, mesh=mesh, in_specs=in_specs, out_specs=out_specs, check_vma=False)
```

```python
import functools

import jax
import jax.numpy as jnp
from jax import lax
from jax.experimental import pallas as pl
from jax.experimental.pallas import tpu as pltpu
from jax.sharding import PartitionSpec as P

MESH = pl.DeviceIdType.MESH


def kernel(
    positions, toks, layers,
    x_ref, enc_ref, enc_bias_ref, dec_ref, dec_bias_ref, out_ref,
    x_buf, enc_buf, dec_buf, lat_buf, y_buf,
    own_sem, recv_sem, right_sem, left_sem, sibling_sem,
    x_send, x_recv, lat_send, lat_recv, y_send, y_recv,
):
    groups = positions // layers
    chips = toks // 2
    me = lax.axis_index("layer")
    tok = lax.axis_index("tok")
    chip, core = tok // 2, tok % 2
    sibling = chip * 2 + 1 - core
    own_layer = me // groups
    enc_rows = enc_ref.shape[1]
    dec_rows = dec_ref.shape[1]
    subs, _, _, sub = dec_buf.shape
    width = subs * sub
    chunks = subs + 1
    has_left, has_right = chip > 0, chip < chips - 1

    folded = chips >= 4
    lowest, highest = (1, chips - 2) if folded else (0, chips - 1)
    is_worker = jnp.logical_and(chip >= lowest, chip <= highest)
    is_end = jnp.logical_not(is_worker)
    paired = jnp.logical_or(chip <= 1, chip >= chips - 2) if folded else chip < 0
    is_helper = jnp.logical_and(paired, is_worker)
    outwards = jnp.logical_or(chip == 0, chip == chips - 2)
    partner = tok + jnp.where(outwards, 2, -2)
    can_left, can_right = chip > lowest, chip < highest

    barrier = pltpu.get_barrier_semaphore()

    def greet(to):
        pl.semaphore_signal(barrier, inc=1, device_id=to, device_id_type=MESH)

    greet((me, sibling))
    for step in range(1, positions):
        greet((lax.rem(me + step, positions), tok))

    def part(chunk, slot):
        if chunk == 0:
            return enc_buf.at[pl.ds(pl.multiple_of(slot * enc_rows, enc_rows), enc_rows), :]
        rows = pl.ds(pl.multiple_of(slot * dec_rows, dec_rows), dec_rows)
        return dec_buf.at[chunk - 1, :, rows, :]

    def load(chunk):
        if chunk == 0:
            source = enc_ref.at[own_layer]
        else:
            columns = pl.ds(pl.multiple_of(me * width + (chunk - 1) * sub, sub), sub)
            source = dec_ref.at[:, :, columns]
        return pltpu.make_async_copy(source, part(chunk, tok), own_sem.at[chunk])

    def send(chunk, slot, to, sems):
        return pltpu.make_async_remote_copy(
            src_ref=part(chunk, slot),
            dst_ref=part(chunk, slot),
            send_sem=sems.at[chunk, slot],
            recv_sem=recv_sem.at[chunk, slot],
            device_id=(me, to),
            device_id_type=MESH,
        )

    def to_right(chunk, slot):
        return send(chunk, slot, tok + 2, right_sem)

    def to_left(chunk, slot):
        return send(chunk, slot, tok - 2, left_sem)

    def to_sibling(chunk, slot):
        return send(chunk, slot, sibling, sibling_sem)

    def to_partner(chunk):
        return send(chunk, tok, partner, right_sem)

    def x_copy():
        return pltpu.make_async_remote_copy(
            src_ref=x_ref,
            dst_ref=x_buf,
            send_sem=x_send.at[0],
            recv_sem=x_recv.at[0],
            device_id=(me, partner),
            device_id_type=MESH,
        )

    for chunk in range(chunks):
        load(chunk).start()

    @pl.when(paired)
    def _():
        for step in range(1, positions):
            greet((lax.rem(me + step, positions), partner))

    @pl.when(has_left)
    def _():
        greet((me, tok - 2))

    @pl.when(has_right)
    def _():
        greet((me, tok + 2))

    neighbours = has_left.astype(jnp.int32) + has_right.astype(jnp.int32)
    crossing = paired.astype(jnp.int32) * (positions - 1)
    pl.semaphore_wait(barrier, positions + neighbours + crossing)

    def start_own(chunk):
        load(chunk).wait()

        @pl.when(can_right)
        def _():
            to_right(chunk, tok).start()

        @pl.when(can_left)
        def _():
            to_left(chunk, tok).start()

        to_sibling(chunk, tok).start()

    def forward(chunk):
        def step(distance, carry):
            @pl.when(chip - distance >= 0)
            def _():
                slot = tok - 2 * distance
                to_sibling(chunk, slot).wait_recv()

                @pl.when(can_right)
                def _():
                    to_right(chunk, slot).start()

                to_sibling(chunk, slot).start()

            @pl.when(chip + distance < chips)
            def _():
                slot = tok + 2 * distance
                to_sibling(chunk, slot).wait_recv()

                @pl.when(can_left)
                def _():
                    to_left(chunk, slot).start()

                to_sibling(chunk, slot).start()

            return carry

        lax.fori_loop(1, chips, step, 0)

    def wait_sibling(chunk):
        def step(index, carry):
            to_sibling(chunk, index * 2 + 1 - core).wait_recv()
            return carry

        lax.fori_loop(0, chips, step, 0)

    def drain(chunk):
        def step(index, carry):
            slot = index * 2 + core
            to_sibling(chunk, slot).wait_send()

            @pl.when(jnp.logical_and(can_right, index <= chip))
            def _():
                to_right(chunk, slot).wait_send()

            @pl.when(jnp.logical_and(can_left, index >= chip))
            def _():
                to_left(chunk, slot).wait_send()

            return carry

        lax.fori_loop(0, chips, step, 0)

    def lat_copy(part_of, step):
        return pltpu.make_async_remote_copy(
            src_ref=lat_buf.at[part_of, me],
            dst_ref=lat_buf.at[part_of, me],
            send_sem=lat_send.at[part_of, step],
            recv_sem=lat_recv.at[part_of, step],
            device_id=(lax.rem(me + step, positions), tok),
            device_id_type=MESH,
        )

    def encode(part_of):
        columns = enc_buf.shape[1]
        tile = min(256, columns)
        tokens = x_buf if part_of else x_ref

        def step(index, carry):
            at = pl.ds(pl.multiple_of(index * tile, tile), tile)
            preact = jnp.dot(tokens[...], enc_buf[:, at], preferred_element_type=jnp.float32)
            preact = preact + enc_bias_ref[pl.ds(own_layer, 1), at]
            lat_buf[part_of, me, :, at] = jnp.maximum(preact, 0.0).astype(lat_buf.dtype)
            return carry

        lax.fori_loop(0, columns // tile, step, 0)
        for step in range(1, positions):
            lat_copy(part_of, step).start()

    group, rank = me // layers, me % layers

    def y_dest(target):
        return target * groups + group

    def columns_of(slot, index):
        return pl.ds(pl.multiple_of(slot * width + index * sub, sub), sub)

    def y_copy(part_of, target, index):
        return pltpu.make_async_remote_copy(
            src_ref=y_buf.at[part_of, target, index],
            dst_ref=out_ref.at[:, :, columns_of(rank, index)],
            send_sem=y_send.at[part_of, target, index],
            recv_sem=y_recv.at[rank, index],
            device_id=(y_dest(target), partner if part_of else tok),
            device_id_type=MESH,
        )

    def y_keep(target, index):
        return pltpu.make_async_copy(
            y_buf.at[0, target, index],
            out_ref.at[:, :, columns_of(rank, index)],
            y_send.at[0, target, index],
        )

    def decode(part_of, target, at):
        first = target * (target + 1) // 2

        def step(index, carry):
            total = jnp.zeros((y_buf.shape[4], sub), jnp.float32)
            for source in range(target + 1):
                total = total + jnp.dot(
                    lat_buf[part_of, source * groups + index],
                    dec_buf[at, first + source],
                    preferred_element_type=jnp.float32,
                )
            total = total + dec_bias_ref[target : target + 1, columns_of(me, at)]
            y_buf[part_of, target, at, index] = total.astype(y_buf.dtype)
            return carry

        lax.fori_loop(0, groups, step, 0)

        if part_of:
            y_copy(part_of, target, at).start()
            return

        @pl.when(y_dest(target) == me)
        def _():
            y_keep(target, at).start()

        @pl.when(y_dest(target) != me)
        def _():
            y_copy(part_of, target, at).start()

    def compute(chunk, part_of):
        if chunk == 0:
            if part_of:
                x_copy().wait_recv()
            encode(part_of)
            return
        if chunk == 1:
            for step in range(1, positions):
                lat_copy(part_of, step).wait_recv()
        for target in range(layers):
            decode(part_of, target, chunk - 1)

    def compute_both(chunk):
        wait_sibling(chunk)
        compute(chunk, 0)

        @pl.when(is_helper)
        def _():
            compute(chunk, 1)

    @pl.when(is_end)
    def _():
        sends = [to_partner(0), x_copy()] + [to_partner(chunk) for chunk in range(1, chunks)]
        loads = [load(0), None] + [load(chunk) for chunk in range(1, chunks)]
        for index in range(chunks + 1):
            if index >= 2:
                sends[index - 2].wait_send()
            if loads[index] is not None:
                loads[index].wait()
            sends[index].start()
        sends[chunks - 1].wait_send()
        sends[chunks].wait_send()

    @pl.when(is_worker)
    def _():
        start_own(0)
        begun = 1
        for chunk in range(chunks):
            ahead = min(chunks, chunk + (2 if chunk == 0 else 3))
            for later in range(begun, ahead):
                start_own(later)
            begun = max(begun, ahead)
            forward(chunk)
            if chunk == 1:
                compute_both(0)
        for chunk in range(0 if chunks <= 1 else 1, chunks):
            compute_both(chunk)

        for target in range(layers):
            for index in range(subs):
                @pl.when(y_dest(target) == me)
                def _():
                    y_keep(target, index).wait()

                @pl.when(y_dest(target) != me)
                def _():
                    y_copy(0, target, index).wait_send()

    for slot in range(layers):
        @pl.when(jnp.logical_or(is_end, lax.rem(me, groups) * layers + slot != me))
        def _():
            for index in range(subs):
                pltpu.make_async_remote_copy(
                    src_ref=y_buf.at[0, 0, index],
                    dst_ref=out_ref.at[:, :, columns_of(slot, index)],
                    send_sem=y_send.at[0, 0, index],
                    recv_sem=y_recv.at[slot, index],
                    device_id=(lax.rem(me + 1, positions), tok),
                    device_id_type=MESH,
                ).wait_recv()

    @pl.when(is_worker)
    def _():
        for step in range(1, positions):
            lat_copy(0, step).wait_send()
        for chunk in range(chunks):
            drain(chunk)

    @pl.when(is_helper)
    def _():
        for step in range(1, positions):
            lat_copy(1, step).wait_send()
        for target in range(layers):
            for index in range(subs):
                y_copy(1, target, index).wait_send()


def body(inputs, enc_weight, enc_bias, dec_weight, dec_bias):
    layers, enc_rows, latent_count = enc_weight.shape
    pairs, dec_rows, features = dec_weight.shape
    positions, toks = lax.axis_size("layer"), lax.axis_size("tok")
    groups = positions // layers
    tok_count = inputs.shape[1]
    width = features // positions
    sub = min(128, width)
    subs = width // sub
    chunks = subs + 1
    vmem = pl.BlockSpec(memory_space=pltpu.VMEM)
    hbm = pl.BlockSpec(memory_space=pltpu.HBM)
    dma = pltpu.SemaphoreType.DMA
    out = pl.pallas_call(
        functools.partial(kernel, positions, toks, layers),
        out_shape=jax.ShapeDtypeStruct((groups, tok_count, layers * width), jnp.bfloat16),
        in_specs=[vmem, hbm, vmem, hbm, vmem],
        out_specs=vmem,
        scratch_shapes=[
            pltpu.VMEM((tok_count, enc_rows * toks), jnp.bfloat16),
            pltpu.VMEM((enc_rows * toks, latent_count), jnp.bfloat16),
            pltpu.VMEM((subs, pairs, dec_rows * toks, sub), jnp.bfloat16),
            pltpu.VMEM((2, positions, tok_count, latent_count), jnp.bfloat16),
            pltpu.VMEM((2, layers, subs, groups, tok_count, sub), jnp.bfloat16),
            dma((chunks,)),
            dma((chunks, toks)),
            dma((chunks, toks)),
            dma((chunks, toks)),
            dma((chunks, toks)),
            dma((1,)),
            dma((1,)),
            dma((2, positions)),
            dma((2, positions)),
            dma((2, layers, subs)),
            dma((layers, subs)),
        ],
        compiler_params=pltpu.CompilerParams(
            collective_id=0, has_side_effects=True, vmem_limit_bytes=58 * 1024 * 1024
        ),
        cost_estimate=pl.CostEstimate(
            flops=2 * tok_count * latent_count * features * (1 + pairs // layers),
            bytes_accessed=8 * 1024 * 1024,
            transcendentals=0,
        ),
    )(inputs[0], enc_weight, enc_bias, dec_weight, dec_bias)
    return out[None]


def solution(mesh):
    in_specs = (P("layer", "tok", None), P(None, "tok", None), P(), P(None, "tok", None), P())
    out_specs = P("layer", None, "tok", None)
    return jax.shard_map(body, mesh=mesh, in_specs=in_specs, out_specs=out_specs, check_vma=False)
```

```python
import functools

import jax
import jax.numpy as jnp
from jax import lax
from jax.experimental import pallas as pl
from jax.experimental.pallas import tpu as pltpu
from jax.sharding import PartitionSpec as P

MESH = pl.DeviceIdType.MESH


def kernel(
    positions, toks, layers,
    x_ref, enc_ref, enc_bias_ref, dec_ref, dec_bias_ref, out_ref,
    x_buf, enc_buf, dec_buf, lat_buf, y_buf,
    own_sem, recv_sem, right_sem, left_sem, sibling_sem,
    x_send, x_recv, lat_send, lat_recv, y_send, y_recv,
):
    groups = positions // layers
    chips = toks // 2
    me = lax.axis_index("layer")
    tok = lax.axis_index("tok")
    chip, core = tok // 2, tok % 2
    sibling = chip * 2 + 1 - core
    own_layer = me // groups
    enc_rows = enc_ref.shape[1]
    dec_rows = dec_ref.shape[1]
    subs, _, _, sub = dec_buf.shape
    width = subs * sub
    chunks = subs + 1
    has_left, has_right = chip > 0, chip < chips - 1

    folded = chips >= 4
    lowest, highest = (1, chips - 2) if folded else (0, chips - 1)
    is_worker = jnp.logical_and(chip >= lowest, chip <= highest)
    is_end = jnp.logical_not(is_worker)
    paired = jnp.logical_or(chip <= 1, chip >= chips - 2) if folded else chip < 0
    is_helper = jnp.logical_and(paired, is_worker)
    outwards = jnp.logical_or(chip == 0, chip == chips - 2)
    partner = tok + jnp.where(outwards, 2, -2)
    can_left, can_right = chip > lowest, chip < highest

    barrier = pltpu.get_barrier_semaphore()

    def greet(to):
        pl.semaphore_signal(barrier, inc=1, device_id=to, device_id_type=MESH)

    greet((me, sibling))
    for step in range(1, positions):
        greet((lax.rem(me + step, positions), tok))

    def part(chunk, slot):
        if chunk == 0:
            return enc_buf.at[pl.ds(pl.multiple_of(slot * enc_rows, enc_rows), enc_rows), :]
        rows = pl.ds(pl.multiple_of(slot * dec_rows, dec_rows), dec_rows)
        return dec_buf.at[chunk - 1, :, rows, :]

    def load(chunk):
        if chunk == 0:
            source = enc_ref.at[own_layer]
        else:
            columns = pl.ds(pl.multiple_of(me * width + (chunk - 1) * sub, sub), sub)
            source = dec_ref.at[:, :, columns]
        return pltpu.make_async_copy(source, part(chunk, tok), own_sem.at[chunk])

    def send(chunk, slot, to, sems):
        return pltpu.make_async_remote_copy(
            src_ref=part(chunk, slot),
            dst_ref=part(chunk, slot),
            send_sem=sems.at[chunk, slot],
            recv_sem=recv_sem.at[chunk, slot],
            device_id=(me, to),
            device_id_type=MESH,
        )

    def to_right(chunk, slot):
        return send(chunk, slot, tok + 2, right_sem)

    def to_left(chunk, slot):
        return send(chunk, slot, tok - 2, left_sem)

    def to_sibling(chunk, slot):
        return send(chunk, slot, sibling, sibling_sem)

    def to_partner(chunk):
        return send(chunk, tok, partner, right_sem)

    def x_copy():
        return pltpu.make_async_remote_copy(
            src_ref=x_ref,
            dst_ref=x_buf,
            send_sem=x_send.at[0],
            recv_sem=x_recv.at[0],
            device_id=(me, partner),
            device_id_type=MESH,
        )

    for chunk in range(chunks):
        load(chunk).start()

    @pl.when(paired)
    def _():
        for step in range(1, positions):
            greet((lax.rem(me + step, positions), partner))

    @pl.when(has_left)
    def _():
        greet((me, tok - 2))

    @pl.when(has_right)
    def _():
        greet((me, tok + 2))

    neighbours = has_left.astype(jnp.int32) + has_right.astype(jnp.int32)
    crossing = paired.astype(jnp.int32) * (positions - 1)
    pl.semaphore_wait(barrier, positions + neighbours + crossing)

    def start_own(chunk):
        load(chunk).wait()

        @pl.when(can_right)
        def _():
            to_right(chunk, tok).start()

        @pl.when(can_left)
        def _():
            to_left(chunk, tok).start()

        to_sibling(chunk, tok).start()

    def forward(chunk):
        def step(distance, carry):
            @pl.when(chip - distance >= 0)
            def _():
                slot = tok - 2 * distance
                to_sibling(chunk, slot).wait_recv()

                @pl.when(can_right)
                def _():
                    to_right(chunk, slot).start()

                to_sibling(chunk, slot).start()

            @pl.when(chip + distance < chips)
            def _():
                slot = tok + 2 * distance
                to_sibling(chunk, slot).wait_recv()

                @pl.when(can_left)
                def _():
                    to_left(chunk, slot).start()

                to_sibling(chunk, slot).start()

            return carry

        lax.fori_loop(1, chips, step, 0)

    def wait_sibling(chunk):
        def step(index, carry):
            to_sibling(chunk, index * 2 + 1 - core).wait_recv()
            return carry

        lax.fori_loop(0, chips, step, 0)

    def drain(chunk):
        def step(index, carry):
            slot = index * 2 + core
            to_sibling(chunk, slot).wait_send()

            @pl.when(jnp.logical_and(can_right, index <= chip))
            def _():
                to_right(chunk, slot).wait_send()

            @pl.when(jnp.logical_and(can_left, index >= chip))
            def _():
                to_left(chunk, slot).wait_send()

            return carry

        lax.fori_loop(0, chips, step, 0)

    def lat_copy(part_of, step):
        return pltpu.make_async_remote_copy(
            src_ref=lat_buf.at[part_of, me],
            dst_ref=lat_buf.at[part_of, me],
            send_sem=lat_send.at[part_of, step],
            recv_sem=lat_recv.at[part_of, step],
            device_id=(lax.rem(me + step, positions), tok),
            device_id_type=MESH,
        )

    def encode(part_of):
        columns = enc_buf.shape[1]
        tile = min(256, columns)
        tokens = x_buf if part_of else x_ref

        def step(index, carry):
            at = pl.ds(pl.multiple_of(index * tile, tile), tile)
            preact = jnp.dot(tokens[...], enc_buf[:, at], preferred_element_type=jnp.float32)
            preact = preact + enc_bias_ref[pl.ds(own_layer, 1), at]
            lat_buf[part_of, me, :, at] = jnp.maximum(preact, 0.0).astype(lat_buf.dtype)
            return carry

        lax.fori_loop(0, columns // tile, step, 0)
        for step in range(1, positions):
            lat_copy(part_of, step).start()

    group, rank = me // layers, me % layers

    def y_dest(target):
        return target * groups + group

    def columns_of(slot, index):
        return pl.ds(pl.multiple_of(slot * width + index * sub, sub), sub)

    def y_copy(part_of, target, index):
        return pltpu.make_async_remote_copy(
            src_ref=y_buf.at[part_of, target, index],
            dst_ref=out_ref.at[:, :, columns_of(rank, index)],
            send_sem=y_send.at[part_of, target, index],
            recv_sem=y_recv.at[rank, index],
            device_id=(y_dest(target), partner if part_of else tok),
            device_id_type=MESH,
        )

    def y_keep(target, index):
        return pltpu.make_async_copy(
            y_buf.at[0, target, index],
            out_ref.at[:, :, columns_of(rank, index)],
            y_send.at[0, target, index],
        )

    def decode(part_of, target, at):
        first = target * (target + 1) // 2

        def step(index, carry):
            total = jnp.zeros((y_buf.shape[4], sub), jnp.float32)
            for source in range(target + 1):
                total = total + jnp.dot(
                    lat_buf[part_of, source * groups + index],
                    dec_buf[at, first + source],
                    preferred_element_type=jnp.float32,
                )
            total = total + dec_bias_ref[target : target + 1, columns_of(me, at)]
            y_buf[part_of, target, at, index] = total.astype(y_buf.dtype)
            return carry

        lax.fori_loop(0, groups, step, 0)

        if part_of:
            y_copy(part_of, target, at).start()
            return

        @pl.when(y_dest(target) == me)
        def _():
            y_keep(target, at).start()

        @pl.when(y_dest(target) != me)
        def _():
            y_copy(part_of, target, at).start()

    def compute(chunk, part_of):
        if chunk == 0:
            if part_of:
                x_copy().wait_recv()
            encode(part_of)
            return
        if chunk == 1:
            for step in range(1, positions):
                lat_copy(part_of, step).wait_recv()
        for target in range(layers):
            decode(part_of, target, chunk - 1)

    def helper_compute(chunk):
        @pl.when(is_helper)
        def _():
            compute(chunk, 1)

    def compute_both(chunk):
        wait_sibling(chunk)
        compute(chunk, 0)
        helper_compute(chunk)

    @pl.when(is_end)
    def _():
        sends = [to_partner(0), x_copy()] + [to_partner(chunk) for chunk in range(1, chunks)]
        loads = [load(0), None] + [load(chunk) for chunk in range(1, chunks)]
        for index in range(chunks + 1):
            if index >= 2:
                sends[index - 2].wait_send()
            if loads[index] is not None:
                loads[index].wait()
            sends[index].start()
        sends[chunks - 1].wait_send()
        sends[chunks].wait_send()

    @pl.when(is_worker)
    def _():
        start_own(0)
        begun = 1
        for chunk in range(chunks):
            ahead = min(chunks, chunk + (2 if chunk == 0 else 3))
            for later in range(begun, ahead):
                start_own(later)
            begun = max(begun, ahead)
            forward(chunk)
            if chunk == 0:
                wait_sibling(0)
                compute(0, 0)
            if chunk == 1:
                helper_compute(0)

        for chunk in range(1, chunks):
            compute_both(chunk)

        for target in range(layers):
            for index in range(subs):
                @pl.when(y_dest(target) == me)
                def _():
                    y_keep(target, index).wait()

                @pl.when(y_dest(target) != me)
                def _():
                    y_copy(0, target, index).wait_send()

    for slot in range(layers):
        @pl.when(jnp.logical_or(is_end, lax.rem(me, groups) * layers + slot != me))
        def _():
            for index in range(subs):
                pltpu.make_async_remote_copy(
                    src_ref=y_buf.at[0, 0, index],
                    dst_ref=out_ref.at[:, :, columns_of(slot, index)],
                    send_sem=y_send.at[0, 0, index],
                    recv_sem=y_recv.at[slot, index],
                    device_id=(lax.rem(me + 1, positions), tok),
                    device_id_type=MESH,
                ).wait_recv()

    @pl.when(is_worker)
    def _():
        for step in range(1, positions):
            lat_copy(0, step).wait_send()
        for chunk in range(chunks):
            drain(chunk)

    @pl.when(is_helper)
    def _():
        for step in range(1, positions):
            lat_copy(1, step).wait_send()
        for target in range(layers):
            for index in range(subs):
                y_copy(1, target, index).wait_send()


def body(inputs, enc_weight, enc_bias, dec_weight, dec_bias):
    layers, enc_rows, latent_count = enc_weight.shape
    pairs, dec_rows, features = dec_weight.shape
    positions, toks = lax.axis_size("layer"), lax.axis_size("tok")
    groups = positions // layers
    tok_count = inputs.shape[1]
    width = features // positions
    sub = min(128, width)
    subs = width // sub
    chunks = subs + 1
    vmem = pl.BlockSpec(memory_space=pltpu.VMEM)
    hbm = pl.BlockSpec(memory_space=pltpu.HBM)
    dma = pltpu.SemaphoreType.DMA
    out = pl.pallas_call(
        functools.partial(kernel, positions, toks, layers),
        out_shape=jax.ShapeDtypeStruct((groups, tok_count, layers * width), jnp.bfloat16),
        in_specs=[vmem, hbm, vmem, hbm, vmem],
        out_specs=vmem,
        scratch_shapes=[
            pltpu.VMEM((tok_count, enc_rows * toks), jnp.bfloat16),
            pltpu.VMEM((enc_rows * toks, latent_count), jnp.bfloat16),
            pltpu.VMEM((subs, pairs, dec_rows * toks, sub), jnp.bfloat16),
            pltpu.VMEM((2, positions, tok_count, latent_count), jnp.bfloat16),
            pltpu.VMEM((2, layers, subs, groups, tok_count, sub), jnp.bfloat16),
            dma((chunks,)),
            dma((chunks, toks)),
            dma((chunks, toks)),
            dma((chunks, toks)),
            dma((chunks, toks)),
            dma((1,)),
            dma((1,)),
            dma((2, positions)),
            dma((2, positions)),
            dma((2, layers, subs)),
            dma((layers, subs)),
        ],
        compiler_params=pltpu.CompilerParams(
            collective_id=0, has_side_effects=True, vmem_limit_bytes=58 * 1024 * 1024
        ),
        cost_estimate=pl.CostEstimate(
            flops=2 * tok_count * latent_count * features * (1 + pairs // layers),
            bytes_accessed=8 * 1024 * 1024,
            transcendentals=0,
        ),
    )(inputs[0], enc_weight, enc_bias, dec_weight, dec_bias)
    return out[None]


def solution(mesh):
    in_specs = (P("layer", "tok", None), P(None, "tok", None), P(), P(None, "tok", None), P())
    out_specs = P("layer", None, "tok", None)
    return jax.shard_map(body, mesh=mesh, in_specs=in_specs, out_specs=out_specs, check_vma=False)
```
